256 devices in a mesh: frames: 32 (over z, x), heads: 2 (over core), dp: 4 (over y).
Axes of the slice: x: 4, y: 4, z: 8, core: 2. Of those that a mesh axis runs over, the one named last changes fastest.
Arguments:
- queries: bfloat16 [4, 1536, 4096], P('dp', 'heads', 'frames'), may hold values from -5.5 to 5.5
- keys: bfloat16 [4, 1536, 4096], P('dp', 'heads', 'frames'), may hold values from -5.5 to 5.5
- values: bfloat16 [4, 1536, 4096], P('dp', 'heads', 'frames'), may hold values from -6 to 6
- grad_out: bfloat16 [4, 1536, 4096], P('dp', 'heads', 'frames'), may hold values from -6 to 6
- out_weight: bfloat16 [1536, 1536], P('heads'), may hold values from -0.15625 to 0.15625
- head_mask: int32 [24], P('heads'), may hold values from 0 to 1, as said below
- lengths: int32 [4], P('dp'), may hold values from 1024 to 4096
- conv_input: bfloat16 [4, 1536, 4096], P('dp', 'heads', 'frames'), may hold values from -6 to 6
- conv_grad: bfloat16 [4, 1536, 4096], P('dp', 'heads', 'frames'), may hold values from -6 to 6
- conv_weight: float32 [31, 1536], P(None, 'heads'), may hold values from -1 to 1
Outputs:
- grad_queries: bfloat16 [4, 1536, 4096], P('dp', 'heads', 'frames')
- grad_keys: bfloat16 [4, 1536, 4096], P('dp', 'heads', 'frames')
- grad_values: bfloat16 [4, 1536, 4096], P('dp', 'heads', 'frames')
- grad_out_weight: float32 [1536, 1536], P('heads')
- grad_conv_input: bfloat16 [4, 1536, 4096], P('dp', 'heads', 'frames')
- grad_conv_weight: float32 [31, 1536], P(None, 'heads')
The draws below stay inside these ranges and needn't reach their ends.
Inputs may be any that keep to these rules, and one draw needn't show every extreme that they name: `head_mask`: exactly 6 heads are pruned.
All inputs are finite; a program needn't handle non-finite values.
Results may differ from the reference program's by a relative error of at most 0.0094.
Values may be sent and summed in bfloat16 or wider, within the bound.
No kernel may reach another device: no remote copies, remote signals or barrier semaphores. Data moves between devices by JAX's collectives and lax.ppermute only.
A program may use at most 192 MiB of HBM per device.

```python
import jax
import jax.numpy as jnp
from jax import lax

D = 1536
HEADS = 24
DH = 64
KW = 31
FRAMES = 4096
BATCH = 4


def draw_queries(key, part):
    key = jax.random.fold_in(key, 1)
    return jnp.clip(jax.random.normal(key, (BATCH, HEADS * DH, FRAMES)), -3.0, 3.0).astype(jnp.bfloat16)


def draw_keys(key, part):
    key = jax.random.fold_in(key, 2)
    return jnp.clip(jax.random.normal(key, (BATCH, HEADS * DH, FRAMES)), -3.0, 3.0).astype(jnp.bfloat16)


def draw_head_mask(key, part):
    key = jax.random.fold_in(key, 3)
    order = jax.random.permutation(key, HEADS)
    return (order >= HEADS // 4).astype(jnp.int32)


def plant(drawn, own_key, smallest, high):
    spot = [jax.random.randint(jax.random.fold_in(own_key, axis), (), 0, length) for axis, length in enumerate(drawn.shape)]
    longest = drawn.shape.index(max(drawn.shape))
    neighbour = spot[:longest] + [(spot[longest] + 1) % drawn.shape[longest]] + spot[longest + 1:]
    return drawn.at[tuple(spot)].set(smallest).at[tuple(neighbour)].set(high)


def steps_of(stream_key, extent, shards, low, high):
    factor_of = 1.0
    for position, shards_of in shards:
        heights = jax.random.uniform(jax.random.fold_in(jax.random.fold_in(stream_key, 6), position), (shards_of,), jnp.float32, low / len(shards), high / len(shards))
        factor_of = factor_of * jnp.repeat(jnp.exp(heights), extent[position] // shards_of).reshape((-1,) + (1,) * (len(extent) - 1 - position))
    return factor_of


def scatter_about(stream_key, shape, deviation, reach, shards=(), dtype=jnp.bfloat16):
    values = jax.random.normal(stream_key, shape, jnp.float32) * deviation
    if len(shards) > 0:
        values = steps_of(stream_key, shape, shards, -0.22, 0.18) * values
    return jnp.clip(values, min=-reach, max=reach).astype(dtype)


def setup_inputs(seed: int = 0) -> dict:
    splits = jax.random.split(jax.random.key(seed), 11)
    queries = draw_queries(jax.random.fold_in(splits[10], 71), 0)
    keys = draw_keys(jax.random.fold_in(splits[10], 71), 0)
    values = scatter_about(splits[2], (BATCH, HEADS * DH, FRAMES), 1.0, 6.0, ((0, 4), (1, 2), (2, 32)))
    grad_out = scatter_about(splits[3], (BATCH, D, FRAMES), 1.0, 6.0, ((0, 4), (1, 2), (2, 32)))
    out_weight = scatter_about(splits[4], (HEADS * DH, D), D ** -0.5, 0.15625, ((0, 2),))
    head_mask = draw_head_mask(jax.random.fold_in(splits[10], 71), 0)
    lengths = plant(jax.random.randint(splits[6], (BATCH,), FRAMES // 4, FRAMES + 1), jax.random.fold_in(splits[6], 1), FRAMES // 4, FRAMES).astype(jnp.int32)
    conv_input = scatter_about(splits[7], (BATCH, D, FRAMES), 1.0, 6.0, ((0, 4), (1, 2), (2, 32)))
    conv_grad = scatter_about(splits[8], (BATCH, D, FRAMES), 1.0, 6.0, ((0, 4), (1, 2), (2, 32)))
    conv_weight = scatter_about(splits[9], (KW, D), KW ** -0.5, 1.0, ((1, 2),), jnp.float32)
    return {"queries": queries, "keys": keys, "values": values, "grad_out": grad_out, "out_weight": out_weight, "head_mask": head_mask, "lengths": lengths, "conv_input": conv_input, "conv_grad": conv_grad, "conv_weight": conv_weight}


def head_grads(element):
    query_head, key_head, value_head, grad_head, length = element
    scores = jnp.dot(query_head, key_head.T, preferred_element_type=jnp.float32) * 0.125
    usable = jnp.arange(FRAMES) < length
    highest = jnp.max(jnp.where(usable[None, :], scores, -1e30), axis=1)
    weight_sum = jnp.sum(jnp.where(usable[None, :], jnp.exp(scores - highest[:, None]), 0.0), axis=1)
    log_total = highest + jnp.log(weight_sum)
    probability = jnp.where(usable[None, :], jnp.exp(scores - log_total[:, None]), 0.0)
    rounded = probability.astype(jnp.bfloat16)
    context = jnp.dot(rounded, value_head, preferred_element_type=jnp.float32)
    row_delta = jnp.sum(grad_head.astype(jnp.float32) * context, axis=1)
    grad_prob = jnp.dot(grad_head, value_head.T, preferred_element_type=jnp.float32)
    grad_score = (probability * (grad_prob - row_delta[:, None])).astype(jnp.bfloat16)
    grad_query = jnp.dot(grad_score, key_head, preferred_element_type=jnp.float32) * 0.125
    grad_key = jnp.dot(grad_score.T, query_head, preferred_element_type=jnp.float32) * 0.125
    grad_value = jnp.dot(rounded.T, grad_head, preferred_element_type=jnp.float32)
    return context, grad_query, grad_key, grad_value


def split_heads(array):
    return array.reshape(BATCH, FRAMES, HEADS, DH).transpose(0, 2, 1, 3).reshape(BATCH * HEADS, FRAMES, DH)


def join_heads(array):
    return array.reshape(BATCH, HEADS, FRAMES, DH).transpose(0, 2, 1, 3).reshape(BATCH, FRAMES, HEADS * DH)


def reference(queries, keys, values, grad_out, out_weight, head_mask, lengths, conv_input, conv_grad, conv_weight):
    queries = queries.transpose(0, 2, 1)
    keys = keys.transpose(0, 2, 1)
    values = values.transpose(0, 2, 1)
    grad_out = grad_out.transpose(0, 2, 1)
    conv_input = conv_input.transpose(0, 2, 1)
    conv_grad = conv_grad.transpose(0, 2, 1)
    mask_cols = jnp.repeat(head_mask.astype(jnp.float32), DH)
    grad_ctx = jnp.einsum("btd,hd->bth", grad_out.astype(jnp.float32), out_weight.astype(jnp.float32))
    grad_ctx = (grad_ctx * mask_cols).astype(jnp.bfloat16)
    head_lengths = jnp.repeat(lengths, HEADS)
    context, grad_query, grad_key, grad_value = lax.map(head_grads, (split_heads(queries), split_heads(keys), split_heads(values), split_heads(grad_ctx), head_lengths))
    context_masked = (join_heads(context) * mask_cols).astype(jnp.bfloat16)
    grad_out_weight = jnp.einsum("bth,btd->hd", context_masked.astype(jnp.float32), grad_out.astype(jnp.float32))
    half_width = KW // 2
    padded_input = jnp.pad(conv_input.astype(jnp.float32), ((0, 0), (half_width, half_width), (0, 0)))
    padded_grad = jnp.pad(conv_grad.astype(jnp.float32), ((0, 0), (half_width, half_width), (0, 0)))
    own_grad = conv_grad.astype(jnp.float32)
    grad_input = jnp.zeros((BATCH, FRAMES, D), jnp.float32)
    tap_sums = []
    for tap_index in range(KW):
        begin = 2 * half_width - tap_index
        grad_input = grad_input + conv_weight[tap_index] * padded_grad[:, begin:begin + FRAMES]
        tap_sums.append(jnp.sum(own_grad * padded_input[:, tap_index:tap_index + FRAMES], axis=(0, 1)))
    grad_conv_weight = jnp.stack(tap_sums)
    grad_q_out = join_heads(grad_query).astype(jnp.bfloat16).transpose(0, 2, 1)
    grad_k_out = join_heads(grad_key).astype(jnp.bfloat16).transpose(0, 2, 1)
    grad_v_out = join_heads(grad_value).astype(jnp.bfloat16).transpose(0, 2, 1)
    grad_in_out = grad_input.astype(jnp.bfloat16).transpose(0, 2, 1)
    return (grad_q_out, grad_k_out, grad_v_out, grad_out_weight, grad_in_out, grad_conv_weight)
```

```python
import functools
import math

import jax
import jax.numpy as jnp
from jax import lax
from jax.experimental import pallas as pl
from jax.experimental.pallas import tpu as pltpu
from jax.sharding import Mesh, PartitionSpec as P

DH = 64
KW = 31
BF = jnp.bfloat16
F32 = jnp.float32
TWO_SCALE = math.log2(math.e) / 8
QB = 512
KC = 512


def nt(a, b):
    return lax.dot_general(a, b, (((1,), (1,)), ((), ())), preferred_element_type=F32)


def nn(a, b):
    return jnp.dot(a, b, preferred_element_type=F32)


def attention_kernel(
    where_ref, mine, other, mine_q, other_q, xch, ctx_out,
    kt, vt, kn, vn, weights, grad_k, grad_v,
):
    blocks, frames = mine.shape[0], mine.shape[2]
    total = blocks * frames
    step = pl.program_id(0)
    length, core = where_ref[0], where_ref[1]
    chunks = total // KC
    per_chunk = KC // frames

    @pl.when(step == 0)
    def _():
        row = lax.broadcasted_iota(jnp.int32, (frames, DH), 0)
        lane = lax.broadcasted_iota(jnp.int32, (frames, DH), 1)
        ones = jnp.where(lane < 3, 1.0, 0.0).astype(BF)
        for s in range(blocks):
            both = jnp.where(core == 0, mine[s], other[s])
            here = pl.ds(s * frames, frames)
            kn[:, here] = both[:DH]
            vn[:DH, here] = both[DH:]
            turned = both.astype(F32)
            kt[here, :DH] = turned[:DH].T.astype(BF)
            vt[here, :DH] = turned[DH:].T.astype(BF)
            first = ((s % 8) * 4 + s // 8) * frames
            masked = jnp.logical_and(lane == 0, row + first >= length)
            kt[here, DH:] = jnp.where(masked, -1e30, 0.0).astype(BF)
            vt[here, DH:] = ones
        vn[DH:, :] = jnp.ones((vn.shape[0] - DH, total), BF)
        grad_k[...] = jnp.zeros_like(grad_k)
        grad_v[...] = jnp.zeros_like(grad_v)

    sources = QB // frames
    q_parts = [jnp.where(core == 1, mine_q[u], other_q[u]) for u in range(sources)]
    q = jnp.concatenate([p[:DH] for p in q_parts], axis=1)
    g = jnp.concatenate([p[DH:] for p in q_parts], axis=1).astype(F32)
    extra = lax.broadcasted_iota(jnp.int32, (DH, QB), 0)
    q_wide = jnp.concatenate([q, jnp.where(extra == 0, 1.0, 0.0).astype(BF)], axis=0)

    high = jnp.full((1, QB), -1e30, F32)
    highs = []
    sums = jnp.zeros((vn.shape[0], QB), F32)
    for i in range(chunks):
        here = pl.ds(i * KC, KC)
        scores = nn(kt[here, :], q_wide)
        new_high = jnp.maximum(high, jnp.max(scores, axis=0, keepdims=True))
        part = jnp.exp2(scores * TWO_SCALE - new_high * TWO_SCALE).astype(BF)
        weights[here, :] = part
        sums = sums * jnp.exp2((high - new_high) * TWO_SCALE) + nn(vn[:, here], part)
        high = new_high
        highs.append(high)
    inverse = 1.0 / sums[DH : DH + 1]
    context = sums[:DH] * inverse
    grad_q = jnp.zeros((DH, QB), F32)
    for i in range(chunks):
        here = pl.ds(i * KC, KC)
        g_part = (g * (inverse * jnp.exp2((highs[i] - high) * TWO_SCALE))).astype(BF)
        delta = jnp.sum(g_part.astype(F32) * context, axis=0, keepdims=True)
        d0 = delta.astype(BF).astype(F32)
        d1 = (delta - d0).astype(BF).astype(F32)
        d2 = delta - d0 - d1
        rows = jnp.where(
            extra == 0, -d0, jnp.where(extra == 1, -d1, jnp.where(extra == 2, -d2, 0.0))
        )
        g_wide = jnp.concatenate([g_part, rows.astype(BF)], axis=0)
        part = weights[here, :]
        grad_score = (part.astype(F32) * nn(vt[here, :], g_wide)).astype(BF)
        grad_q = grad_q + nn(kn[:, here], grad_score)
        grad_k[here, :] += nt(grad_score, q)
        grad_v[here, :] += nt(part, g_part)
    grad_q = (grad_q * 0.125).astype(BF)
    context = context.astype(BF)
    half = DH // 2
    for u in range(sources):
        cols = slice(u * frames, (u + 1) * frames)
        ctx_out[u] = context[:, cols]
        at = pl.ds(pl.multiple_of(blocks * DH + (step * sources + u) * half, half), half)
        xch[0, at, :] = grad_q[:half, cols]
        xch[1, at, :] = grad_q[half:, cols]

    @pl.when(step == pl.num_programs(0) - 1)
    def _():
        for s in range(blocks):
            here = pl.ds(s * frames, frames)
            to = pl.ds(s * DH, DH)
            xch[0, to, :] = (grad_k[here, :].T * 0.125).astype(BF)
            xch[1, to, :] = grad_v[here, :].T.astype(BF)


def attention(where, mine, other):
    blocks, rows, frames = mine.shape
    total = blocks * frames
    sources = QB // frames
    steps = total // 2 // QB
    flops = 6 * 2 * total * (total // 2) * DH
    whole = pl.BlockSpec((blocks, rows, frames), lambda i, w: (0, 0, 0))
    part = pl.BlockSpec((sources, rows, frames), lambda i, w: (w[1] * steps + i, 0, 0))
    return pl.pallas_call(
        attention_kernel,
        grid_spec=pltpu.PrefetchScalarGridSpec(
            num_scalar_prefetch=1,
            grid=(steps,),
            in_specs=[whole, whole, part, part],
            out_specs=[
                pl.BlockSpec((2, blocks * DH + blocks // 2 * (DH // 2), frames), lambda i, w: (0, 0, 0)),
                pl.BlockSpec((sources, DH, frames), lambda i, w: (i, 0, 0)),
            ],
            scratch_shapes=[
                pltpu.VMEM((total, 2 * DH), BF),
                pltpu.VMEM((total, 2 * DH), BF),
                pltpu.VMEM((DH, total), BF),
                pltpu.VMEM((DH + 16, total), BF),
                pltpu.VMEM((total, QB), BF),
                pltpu.VMEM((total, DH), F32),
                pltpu.VMEM((total, DH), F32),
            ],
        ),
        out_shape=[
            jax.ShapeDtypeStruct((2, blocks * DH + blocks // 2 * (DH // 2), frames), BF),
            jax.ShapeDtypeStruct((blocks // 2, DH, frames), BF),
        ],
        compiler_params=pltpu.CompilerParams(
            dimension_semantics=("arbitrary",), vmem_limit_bytes=48 * 1024 * 1024
        ),
        cost_estimate=pl.CostEstimate(flops=flops, bytes_accessed=4 << 20, transcendentals=total * total // 2),
        name="attention",
    )(where, mine, other, mine, other)


def out_weight_kernel(ctx, grad, out):
    @pl.when(pl.program_id(0) == 0)
    def _():
        out[...] = jnp.zeros_like(out)

    for u in range(ctx.shape[0]):
        out[...] += nt(ctx[u], grad[u])


def out_weight_part(ctx, grad):
    blocks, channels, frames = grad.shape
    each = 4
    return pl.pallas_call(
        out_weight_kernel,
        grid=(blocks // each,),
        in_specs=[
            pl.BlockSpec((each, DH, frames), lambda i: (i, 0, 0)),
            pl.BlockSpec((each, channels, frames), lambda i: (i, 0, 0)),
        ],
        out_specs=pl.BlockSpec((DH, channels), lambda i: (0, 0)),
        out_shape=jax.ShapeDtypeStruct((DH, channels), F32),
        compiler_params=pltpu.CompilerParams(dimension_semantics=("arbitrary",)),
        cost_estimate=pl.CostEstimate(
            flops=2 * blocks * DH * channels * frames, bytes_accessed=7 << 20, transcendentals=0
        ),
        name="out_weight",
    )(ctx, grad)


def with_halo(cells, width):
    frames = cells.shape[2]
    order = [(z, x) for z in range(8) for x in range(4)]
    axes = ("z", "x")
    count = len(order)
    head, tail = cells[:, :, :width], cells[:, :, frames - width :]
    left = lax.ppermute(tail, axes, [(i, i + 1) for i in range(count - 1)])
    right = lax.ppermute(head, axes, [(i + 1, i) for i in range(count - 1)])
    return jnp.concatenate([left, cells, right], axis=2)


def convolution(conv_input, conv_grad, conv_weight):
    frames = conv_grad.shape[1]
    half_width = KW // 2
    rimmed = with_halo(jnp.stack([conv_input, conv_grad]), half_width)
    input_wide = rimmed[0].astype(F32)
    grad_wide = rimmed[1].astype(F32)
    own_grad = conv_grad.astype(F32)
    grad_input = jnp.zeros(own_grad.shape, F32)
    tap_sums = []
    for tap in range(KW):
        begin = 2 * half_width - tap
        grad_input = grad_input + conv_weight[tap][:, None] * grad_wide[:, begin : begin + frames]
        tap_sums.append(jnp.sum(own_grad * input_wide[:, tap : tap + frames], axis=1))
    return grad_input.astype(BF), jnp.stack(tap_sums)


def swap(array):
    return lax.ppermute(array, "c", [(0, 1), (1, 0)])


def to_all(array, axes):
    count = lax.axis_size(axes)
    copies = jnp.broadcast_to(array[None], (count, *array.shape))
    return lax.all_to_all(copies, axes, 0, 0, tiled=True)


def per_device(
    queries, keys, values, grad_out, out_weight, head_mask, lengths, conv_input, conv_grad, conv_weight
):
    heads = out_weight.shape[0] // DH
    frames = queries.shape[2]
    width = heads * DH
    core = lax.axis_index("c")
    wide = ("x", "z")
    blocks = lax.axis_size(wide)

    grad_frames = lax.all_gather(grad_out[0], wide, axis=0, tiled=False)
    grad_full = lax.all_gather(grad_out[0], "c", axis=0, tiled=True)
    mask = jnp.repeat(head_mask.astype(F32), DH)[:, None]
    grad_ctx = (nn(out_weight, grad_full) * mask).astype(BF)

    def by_head(a):
        return a.reshape(heads, DH, frames)

    first = jnp.stack(
        [
            jnp.concatenate([by_head(keys[0]), by_head(values[0])], axis=1),
            jnp.concatenate([by_head(queries[0]), by_head(grad_ctx)], axis=1),
        ]
    )
    by_core = lax.all_to_all(first, "c", 0, 0, tiled=True).reshape(2 * heads, 2 * DH, frames)
    padded = jnp.pad(by_core, ((0, blocks - 2 * heads), (0, 0), (0, 0)))
    mine = lax.all_to_all(padded, wide, 0, 0, tiled=True)
    other = swap(mine)

    where = jnp.stack([lengths[0], core.astype(jnp.int32)])
    xch, ctx = attention(where, mine, other)

    xch = lax.all_to_all(xch, "c", 0, 0, tiled=True)
    key_rows = blocks * DH
    summed = (xch[0, :key_rows].astype(F32) + xch[1, :key_rows].astype(F32)).astype(BF)
    back = jnp.concatenate(
        [
            summed.reshape(blocks, DH, frames),
            xch[:, key_rows:].reshape(blocks, DH // 2, frames),
        ],
        axis=1,
    )
    back = lax.all_to_all(back, wide, 0, 0, tiled=True)[: 2 * heads]
    back = lax.all_to_all(
        back.reshape(2, heads, DH + DH // 2, frames), "c", 0, 0, tiled=True
    )
    grad_keys = back[0, :, :DH].reshape(1, width, frames)
    grad_values = back[1, :, :DH].reshape(1, width, frames)
    grad_queries = jnp.concatenate([back[0, :, DH:], back[1, :, DH:]], axis=1).reshape(
        1, width, frames
    )

    ctx_other = swap(ctx)
    ctx_all = jnp.where(
        core == 0, jnp.concatenate([ctx, ctx_other]), jnp.concatenate([ctx_other, ctx])
    )
    part = out_weight_part(ctx_all, grad_frames).astype(BF)
    cols = width // 2
    pieces = part.reshape(8, 8, 2, cols).transpose(0, 2, 1, 3).reshape(16, 8, cols)
    pieces = lax.all_to_all(pieces, ("x", "y"), 0, 0, tiled=True).reshape(4, 4, 8, cols)
    held = jnp.sum(pieces[:3].astype(F32), axis=1).astype(BF)
    held = to_all(held, "z").transpose(1, 0, 2, 3).reshape(2, heads, 8, cols)
    held = lax.all_to_all(held, "c", 0, 0, tiled=True)
    held = to_all(held, ("x", "y")).reshape(8, 2, 2, heads, 8, cols)
    own_mask = head_mask.astype(F32)[:, None, None, None, None, None]
    grad_out_weight = (held.transpose(3, 0, 4, 2, 1, 5).astype(F32) * own_mask).reshape(width, 2 * width)

    grad_conv_input, conv_part = convolution(conv_input[0], conv_grad[0], conv_weight)
    conv_total = lax.psum(conv_part, ("z", "x", "y"))
    return (
        grad_queries,
        grad_keys,
        grad_values,
        grad_out_weight,
        grad_conv_input[None],
        conv_total,
    )


def solution(mesh):
    fine = Mesh(mesh.devices.reshape(8, 4, 2, 4), ("z", "x", "c", "y"))
    frames = ("z", "x")
    cells = P("y", "c", frames)
    return jax.shard_map(
        per_device,
        mesh=fine,
        in_specs=(
            cells, cells, cells, cells, P("c", None), P("c"), P("y"), cells, cells, P(None, "c"),
        ),
        out_specs=(cells, cells, cells, P("c", None), cells, P(None, "c")),
        check_vma=False,
    )
```

```python
import functools
import math

import jax
import jax.numpy as jnp
from jax import lax
from jax.experimental import pallas as pl
from jax.experimental.pallas import tpu as pltpu
from jax.sharding import Mesh, PartitionSpec as P

DH = 64
KW = 31
BF = jnp.bfloat16
F32 = jnp.float32
TWO_SCALE = math.log2(math.e) / 8
QB = 1024
KC = 512


def nt(a, b):
    return lax.dot_general(a, b, (((1,), (1,)), ((), ())), preferred_element_type=F32)


def nn(a, b):
    return jnp.dot(a, b, preferred_element_type=F32)


def attention_kernel(
    where_ref, mine, other, mine_q, other_q, kept, sent, ctx_out,
    kt, vt, kn, vn, weights, grad_k, grad_v,
):
    blocks, frames = mine.shape[0], mine.shape[2]
    total = blocks * frames
    step = pl.program_id(0)
    length, core = where_ref[0], where_ref[1]
    chunks = total // KC
    per_chunk = KC // frames

    @pl.when(step == 0)
    def _():
        row = lax.broadcasted_iota(jnp.int32, (frames, DH), 0)
        lane = lax.broadcasted_iota(jnp.int32, (frames, DH), 1)
        ones = jnp.where(lane < 3, 1.0, 0.0).astype(BF)
        for s in range(blocks):
            both = jnp.where(core == 0, mine[s], other[s])
            here = pl.ds(s * frames, frames)
            kn[:, here] = both[:DH]
            vn[:DH, here] = both[DH:]
            turned = both.astype(F32)
            kt[here, :DH] = turned[:DH].T.astype(BF)
            vt[here, :DH] = turned[DH:].T.astype(BF)
            masked = jnp.logical_and(lane == 0, row + s * frames >= length)
            kt[here, DH:] = jnp.where(masked, -1e30, 0.0).astype(BF)
            vt[here, DH:] = ones
        vn[DH:, :] = jnp.ones((vn.shape[0] - DH, total), BF)
        grad_k[...] = jnp.zeros_like(grad_k)
        grad_v[...] = jnp.zeros_like(grad_v)

    sources = QB // frames
    q_parts = [jnp.where(core == 1, mine_q[u], other_q[u]) for u in range(sources)]
    q = jnp.concatenate([p[:DH] for p in q_parts], axis=1)
    g = jnp.concatenate([p[DH:] for p in q_parts], axis=1).astype(F32)
    extra = lax.broadcasted_iota(jnp.int32, (DH, QB), 0)
    q_wide = jnp.concatenate([q, jnp.where(extra == 0, 1.0, 0.0).astype(BF)], axis=0)

    high = jnp.full((1, QB), -1e30, F32)
    highs = []
    sums = jnp.zeros((vn.shape[0], QB), F32)
    for i in range(chunks):
        here = pl.ds(i * KC, KC)
        scores = nn(kt[here, :], q_wide)
        new_high = jnp.maximum(high, jnp.max(scores, axis=0, keepdims=True))
        part = jnp.exp2(scores * TWO_SCALE - new_high * TWO_SCALE).astype(BF)
        weights[here, :] = part
        sums = sums * jnp.exp2((high - new_high) * TWO_SCALE) + nn(vn[:, here], part)
        high = new_high
        highs.append(high)
    inverse = 1.0 / sums[DH : DH + 1]
    context = sums[:DH] * inverse
    grad_q = jnp.zeros((DH, QB), F32)
    for i in range(chunks):
        here = pl.ds(i * KC, KC)
        g_part = (g * (inverse * jnp.exp2((highs[i] - high) * TWO_SCALE))).astype(BF)
        delta = jnp.sum(g_part.astype(F32) * context, axis=0, keepdims=True)
        d0 = delta.astype(BF).astype(F32)
        d1 = (delta - d0).astype(BF).astype(F32)
        d2 = delta - d0 - d1
        rows = jnp.where(
            extra == 0, -d0, jnp.where(extra == 1, -d1, jnp.where(extra == 2, -d2, 0.0))
        )
        g_wide = jnp.concatenate([g_part, rows.astype(BF)], axis=0)
        part = weights[here, :]
        grad_score = (part.astype(F32) * nn(vt[here, :], g_wide)).astype(BF)
        grad_q = grad_q + nn(kn[:, here], grad_score)
        grad_k[here, :] += nt(grad_score, q)
        grad_v[here, :] += nt(part, g_part)
    grad_q = (grad_q * 0.125).astype(BF)
    context = context.astype(BF)
    half = DH // 2
    for u in range(sources):
        cols = slice(u * frames, (u + 1) * frames)
        ctx_out[u] = context[:, cols]
        at = pl.ds(pl.multiple_of(blocks * DH + (step * sources + u) * half, half), half)
        low, high_half = grad_q[:half, cols], grad_q[half:, cols]
        kept[at, :] = jnp.where(core == 0, low, high_half)
        sent[at, :] = jnp.where(core == 0, high_half, low)

    @pl.when(step == pl.num_programs(0) - 1)
    def _():
        for s in range(blocks):
            here = pl.ds(s * frames, frames)
            to = pl.ds(s * DH, DH)
            of_key = (grad_k[here, :].T * 0.125).astype(BF)
            of_value = grad_v[here, :].T.astype(BF)
            kept[to, :] = jnp.where(core == 0, of_key, of_value)
            sent[to, :] = jnp.where(core == 0, of_value, of_key)


def attention(where, mine, other):
    blocks, rows, frames = mine.shape
    total = blocks * frames
    sources = QB // frames
    steps = total // 2 // QB
    flops = 6 * 2 * total * (total // 2) * DH
    whole = pl.BlockSpec((blocks, rows, frames), lambda i, w: (0, 0, 0))
    part = pl.BlockSpec((sources, rows, frames), lambda i, w: (w[1] * steps + i, 0, 0))
    return pl.pallas_call(
        attention_kernel,
        grid_spec=pltpu.PrefetchScalarGridSpec(
            num_scalar_prefetch=1,
            grid=(steps,),
            in_specs=[whole, whole, part, part],
            out_specs=[
                pl.BlockSpec((blocks * DH + blocks // 2 * (DH // 2), frames), lambda i, w: (0, 0)),
                pl.BlockSpec((blocks * DH + blocks // 2 * (DH // 2), frames), lambda i, w: (0, 0)),
                pl.BlockSpec((sources, DH, frames), lambda i, w: (i, 0, 0)),
            ],
            scratch_shapes=[
                pltpu.VMEM((total, 2 * DH), BF),
                pltpu.VMEM((total, 2 * DH), BF),
                pltpu.VMEM((DH, total), BF),
                pltpu.VMEM((DH + 16, total), BF),
                pltpu.VMEM((total, QB), BF),
                pltpu.VMEM((total, DH), F32),
                pltpu.VMEM((total, DH), F32),
            ],
        ),
        out_shape=[
            jax.ShapeDtypeStruct((blocks * DH + blocks // 2 * (DH // 2), frames), BF),
            jax.ShapeDtypeStruct((blocks * DH + blocks // 2 * (DH // 2), frames), BF),
            jax.ShapeDtypeStruct((blocks // 2, DH, frames), BF),
        ],
        compiler_params=pltpu.CompilerParams(
            dimension_semantics=("arbitrary",), vmem_limit_bytes=48 * 1024 * 1024
        ),
        cost_estimate=pl.CostEstimate(flops=flops, bytes_accessed=4 << 20, transcendentals=total * total // 2),
        name="attention",
    )(where, mine, other, mine, other)


def out_weight_kernel(ctx, grad, out, total):
    step = pl.program_id(0)

    @pl.when(step == 0)
    def _():
        total[...] = jnp.zeros_like(total)

    for u in range(0, ctx.shape[0], 2):
        total[...] += nt(
            jnp.concatenate([grad[u], grad[u + 1]], axis=1),
            jnp.concatenate([ctx[u], ctx[u + 1]], axis=1),
        )

    @pl.when(step == pl.num_programs(0) - 1)
    def _():
        rows = total[...].T.astype(out.dtype)
        high, wide = out.shape[2], out.shape[3]
        for q in range(out.shape[0]):
            for j in range(out.shape[1]):
                out[q, j] = rows[q * high : (q + 1) * high, j * wide : (j + 1) * wide]


def out_weight_part(ctx, grad):
    blocks, channels, frames = grad.shape
    each = 8
    return pl.pallas_call(
        out_weight_kernel,
        grid=(blocks // each,),
        in_specs=[
            pl.BlockSpec((each, DH, frames), lambda i: (i, 0, 0)),
            pl.BlockSpec((each, channels, frames), lambda i: (i, 0, 0)),
        ],
        out_specs=pl.BlockSpec((4, channels // 128, DH // 4, 128), lambda i: (0, 0, 0, 0)),
        out_shape=jax.ShapeDtypeStruct((4, channels // 128, DH // 4, 128), BF),
        scratch_shapes=[pltpu.VMEM((channels, DH), F32)],
        compiler_params=pltpu.CompilerParams(
            dimension_semantics=("arbitrary",), vmem_limit_bytes=32 * 1024 * 1024
        ),
        cost_estimate=pl.CostEstimate(
            flops=2 * blocks * DH * channels * frames, bytes_accessed=7 << 20, transcendentals=0
        ),
        name="out_weight",
    )(ctx, grad)


def assemble_kernel(core_mask, held, out):
    core = core_mask[0]
    x = pl.program_id(0)
    groups, _, quarters, rows, width = out.shape
    tiles = width // 2 // 128
    for g in range(groups):
        factor = core_mask[1 + g * 4 + x].astype(F32)
        for q in range(quarters):
            for side in range(2):
                first = pl.multiple_of(jnp.where(core == side, 0, width // 2), 128)
                for j in range(tiles):
                    at = ((side * groups + g) * tiles + j) * rows
                    part = held[q, at : at + rows, :].astype(F32) * factor
                    out[g, 0, q, :, pl.ds(first + j * 128, 128)] = part


def assemble(core_mask, held, heads):
    groups, rows = heads // 4, DH // 4
    width = 2 * heads * DH
    out = pl.pallas_call(
        assemble_kernel,
        grid_spec=pltpu.PrefetchScalarGridSpec(
            num_scalar_prefetch=1,
            grid=(4,),
            in_specs=[pl.BlockSpec((4, held.shape[1], 128), lambda i, m: (i, 0, 0))],
            out_specs=pl.BlockSpec((groups, 1, 4, rows, width), lambda i, m: (0, i, 0, 0, 0)),
        ),
        out_shape=jax.ShapeDtypeStruct((groups, 4, 4, rows, width), F32),
        compiler_params=pltpu.CompilerParams(
            dimension_semantics=("arbitrary",), vmem_limit_bytes=32 * 1024 * 1024
        ),
        cost_estimate=pl.CostEstimate(flops=1 << 20, bytes_accessed=7 << 20, transcendentals=0),
        name="assemble",
    )(core_mask, held)
    return out.reshape(heads * DH, width)


def halo(array):
    axes = ("z", "x")
    count = lax.axis_size(axes)
    before = lax.ppermute(array, axes, [(i, i + 1) for i in range(count - 1)])
    after = lax.ppermute(array, axes, [(i + 1, i) for i in range(count - 1)])
    return before, after


def convolution_kernel(before, own, after, weight, out, sums):
    rows, frames = own.shape[1], own.shape[2]
    lane = lax.broadcasted_iota(jnp.int32, (rows, frames), 1)
    column = lax.broadcasted_iota(jnp.int32, (frames, frames), 1)
    mine = [own[i].astype(F32) for i in range(2)]
    rest = [
        jnp.where(lane >= frames // 2, before[i].astype(F32), after[i].astype(F32))
        for i in range(2)
    ]

    def shifted(i, by):
        if by == 0:
            return mine[i]
        inside = pltpu.roll(mine[i], (-by) % frames, 1)
        outside = pltpu.roll(rest[i], (-by) % frames, 1)
        here = lane < frames - by if by > 0 else lane >= -by
        return jnp.where(here, inside, outside)

    total = jnp.zeros((rows, frames), F32)
    tap_sums = jnp.zeros((rows, frames), F32)
    for tap in range(KW):
        by = tap - KW // 2
        total = total + weight[:, tap : tap + 1] * shifted(1, -by)
        product = mine[1] * shifted(0, by)
        high = product.astype(BF)
        low = (product - high.astype(F32)).astype(BF)
        pick = jnp.where(column == tap, 1.0, 0.0).astype(BF)
        tap_sums = tap_sums + nn(high, pick) + nn(low, pick)
    out[...] = total.astype(BF)
    sums[...] = tap_sums


def convolution(before, own, after, weight):
    _, channels, frames = own.shape
    rows = 64
    three = pl.BlockSpec((2, rows, frames), lambda i: (0, i, 0))
    flat = pl.BlockSpec((rows, frames), lambda i: (i, 0))
    return pl.pallas_call(
        convolution_kernel,
        grid=(channels // rows,),
        in_specs=[three, three, three, pl.BlockSpec((rows, weight.shape[1]), lambda i: (i, 0))],
        out_specs=[flat, flat],
        out_shape=[
            jax.ShapeDtypeStruct((channels, frames), BF),
            jax.ShapeDtypeStruct((channels, frames), F32),
        ],
        compiler_params=pltpu.CompilerParams(dimension_semantics=("arbitrary",)),
        cost_estimate=pl.CostEstimate(flops=1 << 30, bytes_accessed=3 << 20, transcendentals=0),
        name="convolution",
    )(before, own, after, weight)


def swap(array):
    return lax.ppermute(array, "c", [(0, 1), (1, 0)])


def to_all(array, axes):
    count = lax.axis_size(axes)
    copies = jnp.broadcast_to(array[None], (count, *array.shape))
    return lax.all_to_all(copies, axes, 0, 0, tiled=True)


def per_device(
    queries, keys, values, grad_out, out_weight, head_mask, lengths, conv_input, conv_grad, conv_weight
):
    heads = out_weight.shape[0] // DH
    frames = queries.shape[2]
    width = heads * DH
    core = lax.axis_index("c")
    is_first = core == 0
    frame_axes = ("z", "x")
    blocks = lax.axis_size(frame_axes)

    conv_own = jnp.stack([conv_input[0], conv_grad[0]])
    before, after = halo(conv_own)
    grad_frames = lax.all_gather(grad_out[0], frame_axes, axis=0, tiled=False)
    grad_full = lax.all_gather(grad_out[0], "c", axis=0, tiled=True)
    mask = jnp.repeat(head_mask.astype(F32), DH)[:, None]
    grad_ctx = (nn(out_weight, grad_full) * mask).astype(BF)

    def by_head(a):
        return a.reshape(heads, DH, frames)

    key_value = jnp.concatenate([by_head(keys[0]), by_head(values[0])], axis=1)
    query_grad = jnp.concatenate([by_head(queries[0]), by_head(grad_ctx)], axis=1)
    theirs = swap(jnp.where(is_first, query_grad, key_value))
    ours = jnp.where(is_first, key_value, query_grad)
    padded = jnp.concatenate(
        [
            jnp.where(is_first, ours, theirs),
            jnp.where(is_first, theirs, ours),
            jnp.zeros((blocks - 2 * heads, 2 * DH, frames), BF),
        ]
    )
    padded, before, after = lax.optimization_barrier((padded, before, after))
    mine = lax.all_to_all(padded, frame_axes, 0, 0, tiled=True)
    conv_rows = jnp.pad(conv_weight, ((0, 1), (0, 0))).T
    grad_conv_input, tap_sums = convolution(before, conv_own, after, conv_rows)
    taps = tap_sums[:, : KW + 1].T.reshape(KW + 1, 4, width // 4)
    taps = jnp.pad(taps, ((0, 0), (0, 0), (0, 256 - width // 4))).reshape(128, 2, 128)
    mine, grad_conv_input, taps = lax.optimization_barrier((mine, grad_conv_input, taps))
    taps = lax.all_to_all(taps, ("z", "x", "y"), 0, 0, tiled=True)
    other = swap(mine)

    where = jnp.stack([lengths[0], core.astype(jnp.int32)])
    kept, sent, ctx = attention(where, mine, other)
    kept, sent, ctx, taps = lax.optimization_barrier((kept, sent, ctx, taps))

    got = swap(sent)
    ctx_other = swap(ctx)
    key_rows = blocks * DH
    summed = (kept[:key_rows].astype(F32) + got[:key_rows].astype(F32)).astype(BF)
    dq_ours, dq_theirs = (
        a[key_rows:].reshape(blocks // 2, DH // 2, frames) for a in (kept, got)
    )
    dq = jnp.concatenate(
        [jnp.where(is_first, dq_ours, dq_theirs), jnp.where(is_first, dq_theirs, dq_ours)]
    )
    back = jnp.concatenate([summed.reshape(blocks, DH, frames), dq], axis=1)
    back = lax.all_to_all(back, frame_axes, 0, 0, tiled=True)
    ours = lax.dynamic_slice_in_dim(back, core * heads, heads, axis=0)
    theirs = swap(lax.dynamic_slice_in_dim(back, (1 - core) * heads, heads, axis=0))
    from_first = jnp.where(is_first, ours, theirs)
    from_second = jnp.where(is_first, theirs, ours)
    grad_keys = from_first[:, :DH].reshape(1, width, frames)
    grad_values = from_second[:, :DH].reshape(1, width, frames)
    grad_queries = jnp.concatenate([from_first[:, DH:], from_second[:, DH:]], axis=1).reshape(
        1, width, frames
    )

    ctx_all = jnp.where(
        is_first, jnp.concatenate([ctx, ctx_other]), jnp.concatenate([ctx_other, ctx])
    )
    part = out_weight_part(ctx_all, grad_frames).reshape(4, -1, 128)
    y = lax.axis_index("y")
    held = lax.dynamic_index_in_dim(part, y, keepdims=False).astype(F32)
    for k in range(1, 4):
        piece = lax.dynamic_index_in_dim(part, (y + k) % 4, keepdims=False)
        held = held + lax.ppermute(piece, "y", [(i, (i + k) % 4) for i in range(4)]).astype(F32)
    tap_row = jnp.sum(taps, axis=0).reshape(-1)[: width // 4]
    tap_high = tap_row.astype(BF)
    tap_low = (tap_row - tap_high.astype(F32)).astype(BF)
    tap_row = jnp.concatenate([tap_high, tap_low]).reshape(-1, 128)
    tap_count = tap_row.shape[0]
    held = jnp.concatenate(
        [held.astype(BF), jnp.pad(tap_row, ((0, 16 - tap_count), (0, 0)))], axis=0
    )
    held = to_all(held, "z")
    part_rows = part.shape[1]
    groups = heads // 4
    ours = lax.dynamic_slice_in_dim(held[:, :part_rows], core * groups, groups, axis=0)
    theirs = swap(lax.dynamic_slice_in_dim(held[:, :part_rows], (1 - core) * groups, groups, axis=0))
    tap_rows = held[:, part_rows : part_rows + tap_count].reshape(-1, 128)
    spread = jnp.concatenate(
        [
            ours.reshape(-1, 128),
            theirs.reshape(-1, 128),
            jnp.pad(tap_rows, ((0, -tap_rows.shape[0] % 16), (0, 0))),
        ]
    )
    held = to_all(spread, ("x", "y"))
    core_mask = jnp.concatenate([where[1:], head_mask])
    grad_out_weight = assemble(core_mask, held, heads)
    first = 2 * groups * part_rows
    tap_rows = held[:, first : first + tap_rows.shape[0]].astype(F32)
    tap_rows = tap_rows.reshape(16, 8, 2, width // 4).sum(axis=2).transpose(1, 0, 2)
    conv_total = tap_rows.reshape(KW + 1, width)[:KW]
    return (
        grad_queries,
        grad_keys,
        grad_values,
        grad_out_weight,
        grad_conv_input[None],
        conv_total,
    )


def solution(mesh):
    fine = Mesh(mesh.devices.reshape(8, 4, 2, 4), ("z", "x", "c", "y"))
    frames = ("z", "x")
    cells = P("y", "c", frames)
    return jax.shard_map(
        per_device,
        mesh=fine,
        in_specs=(
            cells, cells, cells, cells, P("c", None), P("c"), P("y"), cells, cells, P(None, "c"),
        ),
        out_specs=(cells, cells, cells, P("c", None), cells, P(None, "c")),
        check_vma=False,
    )
```

```python
import functools
import math

import jax
import jax.numpy as jnp
from jax import lax
from jax.experimental import pallas as pl
from jax.experimental.pallas import tpu as pltpu
from jax.sharding import Mesh, PartitionSpec as P

DH = 64
KW = 31
BF = jnp.bfloat16
F32 = jnp.float32
TWO_SCALE = math.log2(math.e) / 8
EDGE = 16
GROUPS = 8
QB = 1024
KC = 512


def nt(a, b):
    return lax.dot_general(a, b, (((1,), (1,)), ((), ())), preferred_element_type=F32)


def nn(a, b):
    return jnp.dot(a, b, preferred_element_type=F32)


def attention_kernel(
    where_ref, mine, other, mine_q, other_q, kept, sent, ctx_out,
    kt, vt, kn, vn, weights, grad_k, grad_v,
):
    blocks, frames = mine.shape[0], mine.shape[2]
    total = blocks * frames
    step = pl.program_id(0)
    length, core = where_ref[0], where_ref[1]
    chunks = total // KC
    per_chunk = KC // frames

    @pl.when(step == 0)
    def _():
        row = lax.broadcasted_iota(jnp.int32, (frames, DH), 0)
        lane = lax.broadcasted_iota(jnp.int32, (frames, DH), 1)
        ones = jnp.where(lane < 3, 1.0, 0.0).astype(BF)
        for s in range(blocks):
            both = jnp.where(core == 0, mine[s], other[s])
            here = pl.ds(s * frames, frames)
            kn[:, here] = both[:DH]
            vn[:DH, here] = both[DH:]
            turned = both.astype(F32)
            kt[here, :DH] = turned[:DH].T.astype(BF)
            vt[here, :DH] = turned[DH:].T.astype(BF)
            masked = jnp.logical_and(lane == 0, row + s * frames >= length)
            kt[here, DH:] = jnp.where(masked, -1e30, 0.0).astype(BF)
            vt[here, DH:] = ones
        vn[DH:, :] = jnp.ones((vn.shape[0] - DH, total), BF)
        grad_k[...] = jnp.zeros_like(grad_k)
        grad_v[...] = jnp.zeros_like(grad_v)

    sources = QB // frames
    q_parts = [jnp.where(core == 1, mine_q[u], other_q[u]) for u in range(sources)]
    q = jnp.concatenate([p[:DH] for p in q_parts], axis=1)
    g = jnp.concatenate([p[DH:] for p in q_parts], axis=1).astype(F32)
    extra = lax.broadcasted_iota(jnp.int32, (DH, QB), 0)
    q_wide = jnp.concatenate([q, jnp.where(extra == 0, 1.0, 0.0).astype(BF)], axis=0)

    high = jnp.full((1, QB), -1e30, F32)
    highs = []
    sums = jnp.zeros((vn.shape[0], QB), F32)
    for i in range(chunks):
        here = pl.ds(i * KC, KC)
        scores = nn(kt[here, :], q_wide)
        new_high = jnp.maximum(high, jnp.max(scores, axis=0, keepdims=True))
        part = jnp.exp2(scores * TWO_SCALE - new_high * TWO_SCALE).astype(BF)
        weights[here, :] = part
        sums = sums * jnp.exp2((high - new_high) * TWO_SCALE) + nn(vn[:, here], part)
        high = new_high
        highs.append(high)
    inverse = 1.0 / sums[DH : DH + 1]
    context = sums[:DH] * inverse
    grad_q = jnp.zeros((DH, QB), F32)
    for i in range(chunks):
        here = pl.ds(i * KC, KC)
        g_part = (g * (inverse * jnp.exp2((highs[i] - high) * TWO_SCALE))).astype(BF)
        delta = jnp.sum(g_part.astype(F32) * context, axis=0, keepdims=True)
        d0 = delta.astype(BF).astype(F32)
        d1 = (delta - d0).astype(BF).astype(F32)
        d2 = delta - d0 - d1
        rows = jnp.where(
            extra == 0, -d0, jnp.where(extra == 1, -d1, jnp.where(extra == 2, -d2, 0.0))
        )
        g_wide = jnp.concatenate([g_part, rows.astype(BF)], axis=0)
        part = weights[here, :]
        grad_score = (part.astype(F32) * nn(vt[here, :], g_wide)).astype(BF)
        grad_q = grad_q + nn(kn[:, here], grad_score)
        grad_k[here, :] += nt(grad_score, q)
        grad_v[here, :] += nt(part, g_part)
    grad_q = (grad_q * 0.125).astype(BF)
    context = context.astype(BF)
    half = DH // 2
    for u in range(sources):
        cols = slice(u * frames, (u + 1) * frames)
        ctx_out[u] = context[:, cols]
        at = pl.ds(pl.multiple_of(blocks * DH + (step * sources + u) * half, half), half)
        low, high_half = grad_q[:half, cols], grad_q[half:, cols]
        kept[at, :] = jnp.where(core == 0, low, high_half)
        sent[at, :] = jnp.where(core == 0, high_half, low)

    @pl.when(step == pl.num_programs(0) - 1)
    def _():
        for s in range(blocks):
            here = pl.ds(s * frames, frames)
            to = pl.ds(s * DH, DH)
            of_key = (grad_k[here, :].T * 0.125).astype(BF)
            of_value = grad_v[here, :].T.astype(BF)
            kept[to, :] = jnp.where(core == 0, of_key, of_value)
            sent[to, :] = jnp.where(core == 0, of_value, of_key)


def attention(where, mine, other):
    blocks, rows, frames = mine.shape
    total = blocks * frames
    sources = QB // frames
    steps = total // 2 // QB
    flops = 6 * 2 * total * (total // 2) * DH
    whole = pl.BlockSpec((blocks, rows, frames), lambda i, w: (0, 0, 0))
    part = pl.BlockSpec((sources, rows, frames), lambda i, w: (w[1] * steps + i, 0, 0))
    return pl.pallas_call(
        attention_kernel,
        grid_spec=pltpu.PrefetchScalarGridSpec(
            num_scalar_prefetch=1,
            grid=(steps,),
            in_specs=[whole, whole, part, part],
            out_specs=[
                pl.BlockSpec((blocks * DH + blocks // 2 * (DH // 2), frames), lambda i, w: (0, 0)),
                pl.BlockSpec((blocks * DH + blocks // 2 * (DH // 2), frames), lambda i, w: (0, 0)),
                pl.BlockSpec((sources, DH, frames), lambda i, w: (i, 0, 0)),
            ],
            scratch_shapes=[
                pltpu.VMEM((total, 2 * DH), BF),
                pltpu.VMEM((total, 2 * DH), BF),
                pltpu.VMEM((DH, total), BF),
                pltpu.VMEM((DH + 16, total), BF),
                pltpu.VMEM((total, QB), BF),
                pltpu.VMEM((total, DH), F32),
                pltpu.VMEM((total, DH), F32),
            ],
        ),
        out_shape=[
            jax.ShapeDtypeStruct((blocks * DH + blocks // 2 * (DH // 2), frames), BF),
            jax.ShapeDtypeStruct((blocks * DH + blocks // 2 * (DH // 2), frames), BF),
            jax.ShapeDtypeStruct((blocks // 2, DH, frames), BF),
        ],
        compiler_params=pltpu.CompilerParams(
            dimension_semantics=("arbitrary",), vmem_limit_bytes=60 * 1024 * 1024
        ),
        cost_estimate=pl.CostEstimate(flops=flops, bytes_accessed=4 << 20, transcendentals=total * total // 2),
        name="attention",
    )(where, mine, other, mine, other)


def out_weight_kernel(where_ref, ctx, ctx_other, grad, out, total):
    step = pl.program_id(0)
    own_half = step == where_ref[1]
    count = grad.shape[0]
    part = nt(
        jnp.concatenate([grad[u] for u in range(count)], axis=1),
        jnp.concatenate([jnp.where(own_half, ctx[u], ctx_other[u]) for u in range(count)], axis=1),
    )

    @pl.when(step == 0)
    def _():
        total[...] = part

    @pl.when(step == 1)
    def _():
        rows = (total[...] + part).T.astype(out.dtype)
        high, wide = out.shape[2], out.shape[3]
        for q in range(out.shape[0]):
            for j in range(out.shape[1]):
                out[q, j] = rows[q * high : (q + 1) * high, j * wide : (j + 1) * wide]


def out_weight_part(where, ctx, ctx_other, grad):
    blocks, channels, frames = grad.shape
    each = blocks // 2
    part = pl.BlockSpec((each, DH, frames), lambda i, w: (0, 0, 0))
    return pl.pallas_call(
        out_weight_kernel,
        grid_spec=pltpu.PrefetchScalarGridSpec(
            num_scalar_prefetch=1,
            grid=(2,),
            in_specs=[
                part,
                part,
                pl.BlockSpec((each, channels, frames), lambda i, w: (i, 0, 0)),
            ],
            out_specs=pl.BlockSpec((4, channels // 128, DH // 4, 128), lambda i, w: (0, 0, 0, 0)),
            scratch_shapes=[pltpu.VMEM((channels, DH), F32)],
        ),
        out_shape=jax.ShapeDtypeStruct((4, channels // 128, DH // 4, 128), BF),
        compiler_params=pltpu.CompilerParams(
            dimension_semantics=("arbitrary",), vmem_limit_bytes=60 * 1024 * 1024
        ),
        cost_estimate=pl.CostEstimate(
            flops=2 * blocks * DH * channels * frames, bytes_accessed=7 << 20, transcendentals=0
        ),
        name="out_weight",
    )(where, ctx, ctx_other, grad)


def assemble_kernel(place, *refs):
    held, out = refs[:-1], refs[-1]
    core, x, y = place[0], place[1], place[2]
    quarter = pl.program_id(0)
    groups, count, _, rows, width = out.shape
    tiles = width // 2 // 128
    away = (y - quarter) % 4
    for k in range(count):
        from_x = (x - k) % count
        for g in range(groups):
            factor = place[3 + g * count + from_x].astype(F32)
            for side in range(2):
                first = pl.multiple_of(jnp.where(core == side, 0, width // 2), 128)
                for j in range(tiles):
                    at = ((side * groups + g) * tiles + j) * rows
                    part = held[k][away, at : at + rows, :].astype(F32) * factor
                    out[g, from_x, 0, :, pl.ds(first + j * 128, 128)] = part


def assemble(place, held, heads):
    groups, rows = heads // 4, DH // 4
    width = 2 * heads * DH
    whole = pl.BlockSpec(held[0].shape, lambda i, m: (0, 0, 0))
    out = pl.pallas_call(
        assemble_kernel,
        grid_spec=pltpu.PrefetchScalarGridSpec(
            num_scalar_prefetch=1,
            grid=(4,),
            in_specs=[whole] * 4,
            out_specs=pl.BlockSpec((groups, 4, 1, rows, width), lambda i, m: (0, 0, i, 0, 0)),
        ),
        out_shape=jax.ShapeDtypeStruct((groups, 4, 4, rows, width), F32),
        compiler_params=pltpu.CompilerParams(
            dimension_semantics=("arbitrary",), vmem_limit_bytes=32 * 1024 * 1024
        ),
        cost_estimate=pl.CostEstimate(flops=1 << 20, bytes_accessed=7 << 20, transcendentals=0),
        name="assemble",
    )(place, *held)
    return out.reshape(heads * DH, width)


def pack_kernel(conv_input, conv_grad, tails, heads):
    frames = conv_input.shape[1]
    rows = conv_input.shape[0] // GROUPS
    lane = lax.broadcasted_iota(jnp.int32, (rows, frames), 1)
    for i, own in enumerate((conv_input, conv_grad)):
        tail = jnp.zeros((rows, frames), F32)
        head = jnp.zeros((rows, frames), F32)
        for g in range(GROUPS):
            here = own[g * rows : (g + 1) * rows, :].astype(F32)
            group = lane // EDGE == g
            tail = jnp.where(group, pltpu.roll(here, (g + 1) * EDGE % frames, 1), tail)
            head = jnp.where(group, pltpu.roll(here, g * EDGE, 1) if g else here, head)
        tails[i] = tail.astype(BF)
        heads[i] = head.astype(BF)


def halo(conv_input, conv_grad):
    channels, frames = conv_input.shape
    packed = jax.ShapeDtypeStruct((2, channels // GROUPS, frames), BF)
    tails, heads = pl.pallas_call(pack_kernel, out_shape=[packed, packed], name="pack_edges")(
        conv_input, conv_grad
    )
    axes = ("z", "x")
    count = lax.axis_size(axes)
    before = lax.ppermute(tails, axes, [(i, i + 1) for i in range(count - 1)])
    after = lax.ppermute(heads, axes, [(i + 1, i) for i in range(count - 1)])
    return before, after, tails


def shifter(before, own, after, group):
    rows, frames = own.shape
    lane = lax.broadcasted_iota(jnp.int32, (rows, frames), 1)
    rest = jnp.where(
        lane >= frames // 2,
        pltpu.roll(before.astype(F32), frames - (group + 1) * EDGE, 1),
        pltpu.roll(after.astype(F32), (frames - group * EDGE) % frames, 1),
    )
    mine = own.astype(F32)

    def shifted(by):
        if by == 0:
            return mine
        inside = pltpu.roll(mine, (-by) % frames, 1)
        outside = pltpu.roll(rest, (-by) % frames, 1)
        return jnp.where(lane < frames - by if by > 0 else lane >= -by, inside, outside)

    return shifted


def grad_input_kernel(before, own, after, weight, out):
    shifted = shifter(before[1], own[...], after[1], pl.program_id(0))
    total = jnp.zeros(own.shape, F32)
    for tap in range(KW):
        total = total + weight[:, tap : tap + 1] * shifted(KW // 2 - tap)
    out[...] = total.astype(BF)


def conv_grad_input(before, own, after, weight):
    channels, frames = own.shape
    rows = channels // GROUPS
    edge = pl.BlockSpec((2, rows, frames), lambda i: (0, 0, 0))
    flat = pl.BlockSpec((rows, frames), lambda i: (i, 0))
    return pl.pallas_call(
        grad_input_kernel,
        grid=(GROUPS,),
        in_specs=[edge, flat, edge, pl.BlockSpec((rows, weight.shape[1]), lambda i: (i, 0))],
        out_specs=flat,
        out_shape=jax.ShapeDtypeStruct((channels, frames), BF),
        compiler_params=pltpu.CompilerParams(dimension_semantics=("arbitrary",)),
        cost_estimate=pl.CostEstimate(flops=1 << 32, bytes_accessed=3 << 20, transcendentals=0),
        name="conv_grad_input",
    )(before, own, after, weight)


def tap_sums_kernel(before, conv_input, conv_grad, after, out, high, low, pick):
    channels, frames = conv_input.shape
    rows = channels // GROUPS
    column = lax.broadcasted_iota(jnp.int32, (frames, frames), 1)
    for tap in range(KW):
        pick[pl.ds(tap * frames, frames), :] = jnp.where(column == tap, 1.0, 0.0).astype(BF)

    @pl.loop(0, GROUPS)
    def _(i):
        here = pl.ds(pl.multiple_of(i * rows, rows), rows)
        grad = conv_grad[here, :].astype(F32)
        shifted = shifter(before[0], conv_input[here, :], after[0], i)
        for tap in range(KW):
            product = grad * shifted(tap - KW // 2)
            rounded = product.astype(BF)
            at = pl.ds(tap * frames, frames)
            high[here, at] = rounded
            low[here, at] = (product - rounded.astype(F32)).astype(BF)

    sums = (nn(high[...], pick[...]) + nn(low[...], pick[...])).T
    for j in range(out.shape[1]):
        out[:, j, :] = sums[: out.shape[0], j * 128 : (j + 1) * 128]


def conv_tap_sums(before, conv_input, conv_grad, after):
    channels, frames = conv_input.shape
    return pl.pallas_call(
        tap_sums_kernel,
        out_shape=jax.ShapeDtypeStruct((KW + 1, channels // 128, 128), F32),
        scratch_shapes=[
            pltpu.VMEM((channels, KW * frames), BF),
            pltpu.VMEM((channels, KW * frames), BF),
            pltpu.VMEM((KW * frames, frames), BF),
        ],
        compiler_params=pltpu.CompilerParams(vmem_limit_bytes=48 * 1024 * 1024),
        cost_estimate=pl.CostEstimate(flops=1 << 32, bytes_accessed=3 << 20, transcendentals=0),
        name="conv_tap_sums",
    )(before, conv_input, conv_grad, after)


def swap(array):
    return lax.ppermute(array, "c", [(0, 1), (1, 0)])


def ring_gather(array, axis):
    count = lax.axis_size(axis)
    me = lax.axis_index(axis)

    def shift(a, by):
        return lax.ppermute(a, axis, [(i, (i + by) % count) for i in range(count)])

    near = jnp.stack([shift(array, 1), array, shift(array, -1)])
    low, high = shift(near, 3), shift(near[:2], -3)
    ring = jnp.concatenate([low, near, high])
    return lax.dynamic_slice_in_dim(jnp.concatenate([ring, ring]), (4 - me) % count, count, axis=0)


def to_outputs(back, core):
    is_first = core == 0
    heads = back.shape[0] // 2
    width, frames = heads * DH, back.shape[2]
    ours = lax.dynamic_slice_in_dim(back, core * heads, heads, axis=0)
    theirs = swap(lax.dynamic_slice_in_dim(back, (1 - core) * heads, heads, axis=0))
    from_first = jnp.where(is_first, ours, theirs)
    from_second = jnp.where(is_first, theirs, ours)
    grad_queries = jnp.concatenate([from_first[:, DH:], from_second[:, DH:]], axis=1)
    return tuple(
        a.reshape(1, width, frames)
        for a in (from_first[:, :DH], from_second[:, :DH], grad_queries)
    )


def square_gather(array):
    def shift(a, axis, by):
        return lax.ppermute(a, axis, [(i, (i + by) % 4) for i in range(4)])

    column = jnp.stack([array] + [shift(array, "y", k) for k in range(1, 4)])
    return [column] + [shift(column, "x", k) for k in range(1, 4)]


def ring_gather(array, axis):
    count = lax.axis_size(axis)
    me = lax.axis_index(axis)

    def shift(a, by):
        return lax.ppermute(a, axis, [(i, (i + by) % count) for i in range(count)])

    near = jnp.stack([shift(array, 1), array, shift(array, -1)])
    low, high = shift(near, 3), shift(near[:2], -3)
    ring = jnp.concatenate([low, near, high])
    return lax.dynamic_slice_in_dim(jnp.concatenate([ring, ring]), (4 - me) % count, count, axis=0)


def to_outputs(back, core):
    is_first = core == 0
    heads = back.shape[0] // 2
    width, frames = heads * DH, back.shape[2]
    ours = lax.dynamic_slice_in_dim(back, core * heads, heads, axis=0)
    theirs = swap(lax.dynamic_slice_in_dim(back, (1 - core) * heads, heads, axis=0))
    from_first = jnp.where(is_first, ours, theirs)
    from_second = jnp.where(is_first, theirs, ours)
    grad_queries = jnp.concatenate([from_first[:, DH:], from_second[:, DH:]], axis=1)
    return tuple(
        a.reshape(1, width, frames)
        for a in (from_first[:, :DH], from_second[:, :DH], grad_queries)
    )


def to_all(array, axes):
    count = lax.axis_size(axes)
    copies = jnp.broadcast_to(array[None], (count, *array.shape))
    return lax.all_to_all(copies, axes, 0, 0, tiled=True)


def per_device(
    queries, keys, values, grad_out, out_weight, head_mask, lengths, conv_input, conv_grad, conv_weight
):
    heads = out_weight.shape[0] // DH
    frames = queries.shape[2]
    width = heads * DH
    core = lax.axis_index("c")
    is_first = core == 0
    frame_axes = ("z", "x")
    blocks = lax.axis_size(frame_axes)

    before, after, tails = halo(conv_input[0], conv_grad[0])
    own_grad_out, tails = lax.optimization_barrier((grad_out[0], tails))
    grad_frames = lax.all_gather(grad_out[0], frame_axes, axis=0, tiled=False)
    grad_full = lax.all_gather(own_grad_out, "c", axis=0, tiled=True)
    mask = jnp.repeat(head_mask.astype(F32), DH)[:, None]
    grad_ctx = (nn(out_weight, grad_full) * mask).astype(BF)

    def by_head(a):
        return a.reshape(heads, DH, frames)

    key_value = jnp.concatenate([by_head(keys[0]), by_head(values[0])], axis=1)
    query_grad = jnp.concatenate([by_head(queries[0]), by_head(grad_ctx)], axis=1)
    theirs = swap(jnp.where(is_first, query_grad, key_value))
    ours = jnp.where(is_first, key_value, query_grad)
    padded = jnp.concatenate(
        [
            jnp.where(is_first, ours, theirs),
            jnp.where(is_first, theirs, ours),
            jnp.zeros((blocks - 2 * heads, 2 * DH, frames), BF),
        ]
    )
    padded, before, after = lax.optimization_barrier((padded, before, after))
    mine = lax.all_to_all(padded, frame_axes, 0, 0, tiled=True)
    taps = conv_tap_sums(before, conv_input[0], conv_grad[0], after)
    mine, taps = lax.optimization_barrier((mine, taps))
    other = swap(mine)

    where = jnp.stack([lengths[0], core.astype(jnp.int32)])
    kept, sent, ctx = attention(where, mine, other)

    got = swap(sent)
    ctx_other = swap(ctx)
    part = out_weight_part(where, ctx, ctx_other, grad_frames).reshape(4, -1, 128)
    part_rows = part.shape[1]
    pieces = jnp.concatenate([part, taps.astype(BF).reshape(4, -1, 128)], axis=1)
    key_rows = blocks * DH
    summed = (kept[:key_rows].astype(F32) + got[:key_rows].astype(F32)).astype(BF)
    dq_ours, dq_theirs = (
        a[key_rows:].reshape(blocks // 2, DH // 2, frames) for a in (kept, got)
    )
    dq = jnp.concatenate(
        [jnp.where(is_first, dq_ours, dq_theirs), jnp.where(is_first, dq_theirs, dq_ours)]
    )
    back = jnp.concatenate([summed.reshape(blocks, DH, frames), dq], axis=1)
    y = lax.axis_index("y")
    held = lax.dynamic_index_in_dim(pieces, y, keepdims=False).astype(F32)
    for k in range(1, 4):
        piece = lax.dynamic_index_in_dim(pieces, (y + k) % 4, keepdims=False)
        held = held + lax.ppermute(piece, "y", [(i, (i + k) % 4) for i in range(4)]).astype(F32)
    held = ring_gather(held.astype(BF), "z")
    groups = heads // 4
    ours = lax.dynamic_slice_in_dim(held[:, :part_rows], core * groups, groups, axis=0)
    theirs = swap(lax.dynamic_slice_in_dim(held[:, :part_rows], (1 - core) * groups, groups, axis=0))
    tap_rows = held[:, part_rows:].astype(F32).sum(axis=0).astype(BF)
    spread = jnp.concatenate([ours.reshape(-1, 128), theirs.reshape(-1, 128), tap_rows])
    spread, back, before, after = lax.optimization_barrier((spread, back, before, after))
    back = lax.all_to_all(back, frame_axes, 0, 0, tiled=True)[: 2 * heads]
    held = square_gather(spread)
    conv_rows = jnp.pad(conv_weight, ((0, 1), (0, 0))).T
    grad_conv_input = conv_grad_input(before, conv_grad[0], after, conv_rows)
    grad_keys, grad_values, grad_queries = to_outputs(back, core)
    x = lax.axis_index("x")
    place = jnp.concatenate([jnp.stack([core, x, y]).astype(jnp.int32), head_mask])
    grad_out_weight = assemble(place, held, heads)
    taps = sum(a[:, 2 * groups * part_rows :].astype(F32) for a in held).reshape(4, -1)
    taps = lax.dynamic_slice_in_dim(jnp.concatenate([taps[::-1]] * 2), 3 - y, 4, axis=0)
    conv_total = taps.reshape(KW + 1, width)[:KW]
    return (
        grad_queries,
        grad_keys,
        grad_values,
        grad_out_weight,
        grad_conv_input[None],
        conv_total,
    )


def solution(mesh):
    fine = Mesh(mesh.devices.reshape(8, 4, 2, 4), ("z", "x", "c", "y"))
    frames = ("z", "x")
    cells = P("y", "c", frames)
    return jax.shard_map(
        per_device,
        mesh=fine,
        in_specs=(
            cells, cells, cells, cells, P("c", None), P("c"), P("y"), cells, cells, P(None, "c"),
        ),
        out_specs=(cells, cells, cells, P("c", None), cells, P(None, "c")),
        check_vma=False,
    )
```

```python
import functools
import math

import jax
import jax.numpy as jnp
from jax import lax
from jax.experimental import pallas as pl
from jax.experimental.pallas import tpu as pltpu
from jax.sharding import Mesh, PartitionSpec as P

DH = 64
KW = 31
BF = jnp.bfloat16
F32 = jnp.float32
TWO_SCALE = math.log2(math.e) / 8
EDGE = 16
GROUPS = 8
QB = 1024
KC = 512


def nt(a, b):
    return lax.dot_general(a, b, (((1,), (1,)), ((), ())), preferred_element_type=F32)


def nn(a, b):
    return jnp.dot(a, b, preferred_element_type=F32)


def attention_kernel(
    where_ref, mine, other, mine_q, other_q, kept, sent, ctx_out,
    kt, vt, kn, vn, weights, grad_k, grad_v,
):
    blocks, frames = mine.shape[0], mine.shape[2]
    total = blocks * frames
    step = pl.program_id(0)
    length, core = where_ref[0], where_ref[1]
    chunks = total // KC
    per_chunk = KC // frames

    @pl.when(step == 0)
    def _():
        row = lax.broadcasted_iota(jnp.int32, (frames, DH), 0)
        lane = lax.broadcasted_iota(jnp.int32, (frames, DH), 1)
        ones = jnp.where(lane < 3, 1.0, 0.0).astype(BF)
        for s in range(blocks):
            both = jnp.where(core == 0, mine[s], other[s])
            here = pl.ds(s * frames, frames)
            kn[:, here] = both[:DH]
            vn[:DH, here] = both[DH:]
            turned = both.astype(F32)
            kt[here, :DH] = turned[:DH].T.astype(BF)
            vt[here, :DH] = turned[DH:].T.astype(BF)
            masked = jnp.logical_and(lane == 0, row + s * frames >= length)
            kt[here, DH:] = jnp.where(masked, -1e30, 0.0).astype(BF)
            vt[here, DH:] = ones
        vn[DH:, :] = jnp.ones((vn.shape[0] - DH, total), BF)
        grad_k[...] = jnp.zeros_like(grad_k)
        grad_v[...] = jnp.zeros_like(grad_v)

    sources = QB // frames
    q_parts = [jnp.where(core == 1, mine_q[u], other_q[u]) for u in range(sources)]
    q = jnp.concatenate([p[:DH] for p in q_parts], axis=1)
    g = jnp.concatenate([p[DH:] for p in q_parts], axis=1).astype(F32)
    extra = lax.broadcasted_iota(jnp.int32, (DH, QB), 0)
    q_wide = jnp.concatenate([q, jnp.where(extra == 0, 1.0, 0.0).astype(BF)], axis=0)

    high = jnp.full((1, QB), -1e30, F32)
    highs = []
    sums = jnp.zeros((vn.shape[0], QB), F32)
    for i in range(chunks):
        here = pl.ds(i * KC, KC)
        scores = nn(kt[here, :], q_wide)
        new_high = jnp.maximum(high, jnp.max(scores, axis=0, keepdims=True))
        part = jnp.exp2(scores * TWO_SCALE - new_high * TWO_SCALE).astype(BF)
        weights[here, :] = part
        sums = sums * jnp.exp2((high - new_high) * TWO_SCALE) + nn(vn[:, here], part)
        high = new_high
        highs.append(high)
    inverse = 1.0 / sums[DH : DH + 1]
    context = sums[:DH] * inverse
    grad_q = jnp.zeros((DH, QB), F32)
    for i in range(chunks):
        here = pl.ds(i * KC, KC)
        g_part = (g * (inverse * jnp.exp2((highs[i] - high) * TWO_SCALE))).astype(BF)
        delta = jnp.sum(g_part.astype(F32) * context, axis=0, keepdims=True)
        d0 = delta.astype(BF).astype(F32)
        d1 = (delta - d0).astype(BF).astype(F32)
        d2 = delta - d0 - d1
        rows = jnp.where(
            extra == 0, -d0, jnp.where(extra == 1, -d1, jnp.where(extra == 2, -d2, 0.0))
        )
        g_wide = jnp.concatenate([g_part, rows.astype(BF)], axis=0)
        part = weights[here, :]
        grad_score = (part.astype(F32) * nn(vt[here, :], g_wide)).astype(BF)
        grad_q = grad_q + nn(kn[:, here], grad_score)
        grad_k[here, :] += nt(grad_score, q)
        grad_v[here, :] += nt(part, g_part)
    grad_q = (grad_q * 0.125).astype(BF)
    context = context.astype(BF)
    half = DH // 2
    for u in range(sources):
        cols = slice(u * frames, (u + 1) * frames)
        ctx_out[u] = context[:, cols]
        at = pl.ds(pl.multiple_of(blocks * DH + (step * sources + u) * half, half), half)
        low, high_half = grad_q[:half, cols], grad_q[half:, cols]
        kept[at, :] = jnp.where(core == 0, low, high_half)
        sent[at, :] = jnp.where(core == 0, high_half, low)

    @pl.when(step == pl.num_programs(0) - 1)
    def _():
        for s in range(blocks):
            here = pl.ds(s * frames, frames)
            to = pl.ds(s * DH, DH)
            of_key = (grad_k[here, :].T * 0.125).astype(BF)
            of_value = grad_v[here, :].T.astype(BF)
            kept[to, :] = jnp.where(core == 0, of_key, of_value)
            sent[to, :] = jnp.where(core == 0, of_value, of_key)


def attention(where, mine, other):
    blocks, rows, frames = mine.shape
    total = blocks * frames
    sources = QB // frames
    steps = total // 2 // QB
    flops = 6 * 2 * total * (total // 2) * DH
    whole = pl.BlockSpec((blocks, rows, frames), lambda i, w: (0, 0, 0))
    part = pl.BlockSpec((sources, rows, frames), lambda i, w: (w[1] * steps + i, 0, 0))
    return pl.pallas_call(
        attention_kernel,
        grid_spec=pltpu.PrefetchScalarGridSpec(
            num_scalar_prefetch=1,
            grid=(steps,),
            in_specs=[whole, whole, part, part],
            out_specs=[
                pl.BlockSpec((blocks * DH + blocks // 2 * (DH // 2), frames), lambda i, w: (0, 0)),
                pl.BlockSpec((blocks * DH + blocks // 2 * (DH // 2), frames), lambda i, w: (0, 0)),
                pl.BlockSpec((sources, DH, frames), lambda i, w: (i, 0, 0)),
            ],
            scratch_shapes=[
                pltpu.VMEM((total, 2 * DH), BF),
                pltpu.VMEM((total, 2 * DH), BF),
                pltpu.VMEM((DH, total), BF),
                pltpu.VMEM((DH + 16, total), BF),
                pltpu.VMEM((total, QB), BF),
                pltpu.VMEM((total, DH), F32),
                pltpu.VMEM((total, DH), F32),
            ],
        ),
        out_shape=[
            jax.ShapeDtypeStruct((blocks * DH + blocks // 2 * (DH // 2), frames), BF),
            jax.ShapeDtypeStruct((blocks * DH + blocks // 2 * (DH // 2), frames), BF),
            jax.ShapeDtypeStruct((blocks // 2, DH, frames), BF),
        ],
        compiler_params=pltpu.CompilerParams(
            dimension_semantics=("arbitrary",), vmem_limit_bytes=48 * 1024 * 1024
        ),
        cost_estimate=pl.CostEstimate(flops=flops, bytes_accessed=4 << 20, transcendentals=total * total // 2),
        name="attention",
    )(where, mine, other, mine, other)


def out_weight_kernel(where_ref, ctx, ctx_other, grad, out, total):
    step = pl.program_id(0)
    own_half = step == where_ref[1]
    count = grad.shape[0]
    part = nt(
        jnp.concatenate([grad[u] for u in range(count)], axis=1),
        jnp.concatenate([jnp.where(own_half, ctx[u], ctx_other[u]) for u in range(count)], axis=1),
    )

    @pl.when(step == 0)
    def _():
        total[...] = part

    @pl.when(step == 1)
    def _():
        rows = (total[...] + part).T.astype(out.dtype)
        high, wide = out.shape[2], out.shape[3]
        for q in range(out.shape[0]):
            for j in range(out.shape[1]):
                out[q, j] = rows[q * high : (q + 1) * high, j * wide : (j + 1) * wide]


def out_weight_part(where, ctx, ctx_other, grad):
    blocks, channels, frames = grad.shape
    each = blocks // 2
    part = pl.BlockSpec((each, DH, frames), lambda i, w: (0, 0, 0))
    return pl.pallas_call(
        out_weight_kernel,
        grid_spec=pltpu.PrefetchScalarGridSpec(
            num_scalar_prefetch=1,
            grid=(2,),
            in_specs=[
                part,
                part,
                pl.BlockSpec((each, channels, frames), lambda i, w: (i, 0, 0)),
            ],
            out_specs=pl.BlockSpec((4, channels // 128, DH // 4, 128), lambda i, w: (0, 0, 0, 0)),
            scratch_shapes=[pltpu.VMEM((channels, DH), F32)],
        ),
        out_shape=jax.ShapeDtypeStruct((4, channels // 128, DH // 4, 128), BF),
        compiler_params=pltpu.CompilerParams(
            dimension_semantics=("arbitrary",), vmem_limit_bytes=48 * 1024 * 1024
        ),
        cost_estimate=pl.CostEstimate(
            flops=2 * blocks * DH * channels * frames, bytes_accessed=7 << 20, transcendentals=0
        ),
        name="out_weight",
    )(where, ctx, ctx_other, grad)


def assemble_kernel(place, *refs):
    held, out = refs[:-1], refs[-1]
    core, x, y = place[0], place[1], place[2]
    quarter = pl.program_id(0)
    groups, count, _, rows, width = out.shape
    tiles = width // 2 // 128
    away = (y - quarter) % 4
    for k in range(count):
        from_x = (x - k) % count
        for g in range(groups):
            factor = place[3 + g * count + from_x].astype(F32)
            for side in range(2):
                first = pl.multiple_of(jnp.where(core == side, 0, width // 2), 128)
                for j in range(tiles):
                    at = ((side * groups + g) * tiles + j) * rows
                    part = held[k][away, at : at + rows, :].astype(F32) * factor
                    out[g, from_x, 0, :, pl.ds(first + j * 128, 128)] = part


def assemble(place, held, heads):
    groups, rows = heads // 4, DH // 4
    width = 2 * heads * DH
    whole = pl.BlockSpec(held[0].shape, lambda i, m: (0, 0, 0))
    out = pl.pallas_call(
        assemble_kernel,
        grid_spec=pltpu.PrefetchScalarGridSpec(
            num_scalar_prefetch=1,
            grid=(4,),
            in_specs=[whole] * 4,
            out_specs=pl.BlockSpec((groups, 4, 1, rows, width), lambda i, m: (0, 0, i, 0, 0)),
        ),
        out_shape=jax.ShapeDtypeStruct((groups, 4, 4, rows, width), F32),
        compiler_params=pltpu.CompilerParams(
            dimension_semantics=("arbitrary",), vmem_limit_bytes=32 * 1024 * 1024
        ),
        cost_estimate=pl.CostEstimate(flops=1 << 20, bytes_accessed=7 << 20, transcendentals=0),
        name="assemble",
    )(place, *held)
    return out.reshape(heads * DH, width)


def pack_kernel(conv_input, conv_grad, tails, heads):
    frames = conv_input.shape[1]
    rows = conv_input.shape[0] // GROUPS
    lane = lax.broadcasted_iota(jnp.int32, (rows, frames), 1)
    for i, own in enumerate((conv_input, conv_grad)):
        tail = jnp.zeros((rows, frames), F32)
        head = jnp.zeros((rows, frames), F32)
        for g in range(GROUPS):
            here = own[g * rows : (g + 1) * rows, :].astype(F32)
            group = lane // EDGE == g
            tail = jnp.where(group, pltpu.roll(here, (g + 1) * EDGE % frames, 1), tail)
            head = jnp.where(group, pltpu.roll(here, g * EDGE, 1) if g else here, head)
        tails[i] = tail.astype(BF)
        heads[i] = head.astype(BF)


def halo(conv_input, conv_grad):
    channels, frames = conv_input.shape
    packed = jax.ShapeDtypeStruct((2, channels // GROUPS, frames), BF)
    tails, heads = pl.pallas_call(pack_kernel, out_shape=[packed, packed], name="pack_edges")(
        conv_input, conv_grad
    )
    axes = ("z", "x")
    count = lax.axis_size(axes)
    before = lax.ppermute(tails, axes, [(i, i + 1) for i in range(count - 1)])
    after = lax.ppermute(heads, axes, [(i + 1, i) for i in range(count - 1)])
    return before, after, tails


def shifter(before, own, after, group):
    rows, frames = own.shape
    lane = lax.broadcasted_iota(jnp.int32, (rows, frames), 1)
    rest = jnp.where(
        lane >= frames // 2,
        pltpu.roll(before.astype(F32), frames - (group + 1) * EDGE, 1),
        pltpu.roll(after.astype(F32), (frames - group * EDGE) % frames, 1),
    )
    mine = own.astype(F32)

    def shifted(by):
        if by == 0:
            return mine
        inside = pltpu.roll(mine, (-by) % frames, 1)
        outside = pltpu.roll(rest, (-by) % frames, 1)
        return jnp.where(lane < frames - by if by > 0 else lane >= -by, inside, outside)

    return shifted


def grad_input_kernel(before, own, after, weight, out):
    shifted = shifter(before[1], own[...], after[1], pl.program_id(0))
    total = jnp.zeros(own.shape, F32)
    for tap in range(KW):
        total = total + weight[:, tap : tap + 1] * shifted(KW // 2 - tap)
    out[...] = total.astype(BF)


def conv_grad_input(before, own, after, weight):
    channels, frames = own.shape
    rows = channels // GROUPS
    edge = pl.BlockSpec((2, rows, frames), lambda i: (0, 0, 0))
    flat = pl.BlockSpec((rows, frames), lambda i: (i, 0))
    return pl.pallas_call(
        grad_input_kernel,
        grid=(GROUPS,),
        in_specs=[edge, flat, edge, pl.BlockSpec((rows, weight.shape[1]), lambda i: (i, 0))],
        out_specs=flat,
        out_shape=jax.ShapeDtypeStruct((channels, frames), BF),
        compiler_params=pltpu.CompilerParams(dimension_semantics=("arbitrary",)),
        cost_estimate=pl.CostEstimate(flops=1 << 32, bytes_accessed=3 << 20, transcendentals=0),
        name="conv_grad_input",
    )(before, own, after, weight)


def tap_sums_kernel(before, conv_input, conv_grad, after, out, high, low, pick):
    channels, frames = conv_input.shape
    rows = channels // GROUPS
    column = lax.broadcasted_iota(jnp.int32, (frames, frames), 1)
    for tap in range(KW):
        pick[pl.ds(tap * frames, frames), :] = jnp.where(column == tap, 1.0, 0.0).astype(BF)

    @pl.loop(0, GROUPS)
    def _(i):
        here = pl.ds(pl.multiple_of(i * rows, rows), rows)
        grad = conv_grad[here, :].astype(F32)
        shifted = shifter(before[0], conv_input[here, :], after[0], i)
        for tap in range(KW):
            product = grad * shifted(tap - KW // 2)
            rounded = product.astype(BF)
            at = pl.ds(tap * frames, frames)
            high[here, at] = rounded
            low[here, at] = (product - rounded.astype(F32)).astype(BF)

    sums = (nn(high[...], pick[...]) + nn(low[...], pick[...])).T
    for j in range(out.shape[1]):
        out[:, j, :] = sums[: out.shape[0], j * 128 : (j + 1) * 128]


def conv_tap_sums(before, conv_input, conv_grad, after):
    channels, frames = conv_input.shape
    return pl.pallas_call(
        tap_sums_kernel,
        out_shape=jax.ShapeDtypeStruct((KW + 1, channels // 128, 128), F32),
        scratch_shapes=[
            pltpu.VMEM((channels, KW * frames), BF),
            pltpu.VMEM((channels, KW * frames), BF),
            pltpu.VMEM((KW * frames, frames), BF),
        ],
        compiler_params=pltpu.CompilerParams(vmem_limit_bytes=48 * 1024 * 1024),
        cost_estimate=pl.CostEstimate(flops=1 << 32, bytes_accessed=3 << 20, transcendentals=0),
        name="conv_tap_sums",
    )(before, conv_input, conv_grad, after)


def swap(array):
    return lax.ppermute(array, "c", [(0, 1), (1, 0)])


def ring_gather(array, axis):
    count = lax.axis_size(axis)
    me = lax.axis_index(axis)

    def shift(a, by):
        return lax.ppermute(a, axis, [(i, (i + by) % count) for i in range(count)])

    near = jnp.stack([shift(array, 1), array, shift(array, -1)])
    low, high = shift(near, 3), shift(near[:2], -3)
    ring = jnp.concatenate([low, near, high])
    return lax.dynamic_slice_in_dim(jnp.concatenate([ring, ring]), (4 - me) % count, count, axis=0)


def to_outputs(back, core):
    is_first = core == 0
    heads = back.shape[0] // 2
    width, frames = heads * DH, back.shape[2]
    ours = lax.dynamic_slice_in_dim(back, core * heads, heads, axis=0)
    theirs = swap(lax.dynamic_slice_in_dim(back, (1 - core) * heads, heads, axis=0))
    from_first = jnp.where(is_first, ours, theirs)
    from_second = jnp.where(is_first, theirs, ours)
    grad_queries = jnp.concatenate([from_first[:, DH:], from_second[:, DH:]], axis=1)
    return tuple(
        a.reshape(1, width, frames)
        for a in (from_first[:, :DH], from_second[:, :DH], grad_queries)
    )


def square_gather(array):
    def shift(a, axis, by):
        return lax.ppermute(a, axis, [(i, (i + by) % 4) for i in range(4)])

    column = jnp.stack([array] + [shift(array, "y", k) for k in range(1, 4)])
    return [column] + [shift(column, "x", k) for k in range(1, 4)]


def ring_gather(array, axis):
    count = lax.axis_size(axis)
    me = lax.axis_index(axis)

    def shift(a, by):
        return lax.ppermute(a, axis, [(i, (i + by) % count) for i in range(count)])

    near = jnp.stack([shift(array, 1), array, shift(array, -1)])
    low, high = shift(near, 3), shift(near[:2], -3)
    ring = jnp.concatenate([low, near, high])
    return lax.dynamic_slice_in_dim(jnp.concatenate([ring, ring]), (4 - me) % count, count, axis=0)


def to_outputs(back, core):
    is_first = core == 0
    heads = back.shape[0] // 2
    width, frames = heads * DH, back.shape[2]
    ours = lax.dynamic_slice_in_dim(back, core * heads, heads, axis=0)
    theirs = swap(lax.dynamic_slice_in_dim(back, (1 - core) * heads, heads, axis=0))
    from_first = jnp.where(is_first, ours, theirs)
    from_second = jnp.where(is_first, theirs, ours)
    grad_queries = jnp.concatenate([from_first[:, DH:], from_second[:, DH:]], axis=1)
    return tuple(
        a.reshape(1, width, frames)
        for a in (from_first[:, :DH], from_second[:, :DH], grad_queries)
    )


def to_all(array, axes):
    count = lax.axis_size(axes)
    copies = jnp.broadcast_to(array[None], (count, *array.shape))
    return lax.all_to_all(copies, axes, 0, 0, tiled=True)


def per_device(
    queries, keys, values, grad_out, out_weight, head_mask, lengths, conv_input, conv_grad, conv_weight
):
    heads = out_weight.shape[0] // DH
    frames = queries.shape[2]
    width = heads * DH
    core = lax.axis_index("c")
    is_first = core == 0
    frame_axes = ("z", "x")
    blocks = lax.axis_size(frame_axes)

    before, after, tails = halo(conv_input[0], conv_grad[0])
    own_grad_out, tails = lax.optimization_barrier((grad_out[0], tails))
    grad_frames = lax.all_gather(grad_out[0], frame_axes, axis=0, tiled=False)
    grad_full = lax.all_gather(own_grad_out, "c", axis=0, tiled=True)
    mask = jnp.repeat(head_mask.astype(F32), DH)[:, None]
    grad_ctx = (nn(out_weight, grad_full) * mask).astype(BF)

    def by_head(a):
        return a.reshape(heads, DH, frames)

    key_value = jnp.concatenate([by_head(keys[0]), by_head(values[0])], axis=1)
    query_grad = jnp.concatenate([by_head(queries[0]), by_head(grad_ctx)], axis=1)
    theirs = swap(jnp.where(is_first, query_grad, key_value))
    ours = jnp.where(is_first, key_value, query_grad)
    padded = jnp.concatenate(
        [
            jnp.where(is_first, ours, theirs),
            jnp.where(is_first, theirs, ours),
            jnp.zeros((blocks - 2 * heads, 2 * DH, frames), BF),
        ]
    )
    padded, before, after = lax.optimization_barrier((padded, before, after))
    mine = lax.all_to_all(padded, frame_axes, 0, 0, tiled=True)
    taps = conv_tap_sums(before, conv_input[0], conv_grad[0], after)
    mine, taps = lax.optimization_barrier((mine, taps))
    other = swap(mine)

    where = jnp.stack([lengths[0], core.astype(jnp.int32)])
    kept, sent, ctx = attention(where, mine, other)

    got = swap(sent)
    ctx_other = swap(ctx)
    part = out_weight_part(where, ctx, ctx_other, grad_frames).reshape(4, -1, 128)
    part_rows = part.shape[1]
    pieces = jnp.concatenate([part, taps.astype(BF).reshape(4, -1, 128)], axis=1)
    key_rows = blocks * DH
    summed = (kept[:key_rows].astype(F32) + got[:key_rows].astype(F32)).astype(BF)
    dq_ours, dq_theirs = (
        a[key_rows:].reshape(blocks // 2, DH // 2, frames) for a in (kept, got)
    )
    dq = jnp.concatenate(
        [jnp.where(is_first, dq_ours, dq_theirs), jnp.where(is_first, dq_theirs, dq_ours)]
    )
    back = jnp.concatenate([summed.reshape(blocks, DH, frames), dq], axis=1)
    y = lax.axis_index("y")
    held = lax.dynamic_index_in_dim(pieces, y, keepdims=False).astype(F32)
    for k in range(1, 4):
        piece = lax.dynamic_index_in_dim(pieces, (y + k) % 4, keepdims=False)
        held = held + lax.ppermute(piece, "y", [(i, (i + k) % 4) for i in range(4)]).astype(F32)
    held = ring_gather(held.astype(BF), "z")
    groups = heads // 4
    ours = lax.dynamic_slice_in_dim(held[:, :part_rows], core * groups, groups, axis=0)
    theirs = swap(lax.dynamic_slice_in_dim(held[:, :part_rows], (1 - core) * groups, groups, axis=0))
    tap_rows = held[:, part_rows:].astype(F32).sum(axis=0).astype(BF)
    spread = jnp.concatenate([ours.reshape(-1, 128), theirs.reshape(-1, 128), tap_rows])
    spread, back, before, after = lax.optimization_barrier((spread, back, before, after))
    back = lax.all_to_all(back, frame_axes, 0, 0, tiled=True)[: 2 * heads]
    held = square_gather(spread)
    conv_rows = jnp.pad(conv_weight, ((0, 1), (0, 0))).T
    grad_conv_input = conv_grad_input(before, conv_grad[0], after, conv_rows)
    grad_keys, grad_values, grad_queries = to_outputs(back, core)
    x = lax.axis_index("x")
    place = jnp.concatenate([jnp.stack([core, x, y]).astype(jnp.int32), head_mask])
    grad_out_weight = assemble(place, held, heads)
    taps = sum(a[:, 2 * groups * part_rows :].astype(F32) for a in held).reshape(4, -1)
    taps = lax.dynamic_slice_in_dim(jnp.concatenate([taps[::-1]] * 2), 3 - y, 4, axis=0)
    conv_total = taps.reshape(KW + 1, width)[:KW]
    return (
        grad_queries,
        grad_keys,
        grad_values,
        grad_out_weight,
        grad_conv_input[None],
        conv_total,
    )


def solution(mesh):
    fine = Mesh(mesh.devices.reshape(8, 4, 2, 4), ("z", "x", "c", "y"))
    frames = ("z", "x")
    cells = P("y", "c", frames)
    return jax.shard_map(
        per_device,
        mesh=fine,
        in_specs=(
            cells, cells, cells, cells, P("c", None), P("c"), P("y"), cells, cells, P(None, "c"),
        ),
        out_specs=(cells, cells, cells, P("c", None), cells, P(None, "c")),
        check_vma=False,
    )
```
